1024 devices in a mesh: dp: 8 (over z_lo), expert: 32 (over x, y), tensor: 4 (over z_hi, core).
Axes of the slice: x: 4, y: 8, z: 16 (z_hi: 2, z_lo: 8; z = z_hi * 8 + z_lo), core: 2. Of those that a mesh axis runs over, the one named last changes fastest.
Arguments:
- grad_output: bfloat16 [4096, 4096], P('expert', 'dp'), may hold values from -6 to 6
- gate_probs: float32 [4096, 8], P('expert'), may hold values from 0.05 to 0.6
- routes: int32 [4096, 8], P('expert'), may hold values from 0 to 31, all different within a row; in each aligned block of 128 rows (0 to 127, 128 to 255, ...) at most 40 rows name the same one
- saved_input: bfloat16 [32, 1280, 4096], P('expert', None, 'dp'), may hold values from -6 to 6
- saved_gate: bfloat16 [32, 1280, 1536], P('expert', None, 'tensor'), may hold values from -6 to 6
- saved_up: bfloat16 [32, 1280, 1536], P('expert', None, 'tensor'), may hold values from -6 to 6
- w_gate: bfloat16 [32, 4096, 1536], P('expert', 'dp', 'tensor'), may hold values from -0.09375 to 0.09375
- w_up: bfloat16 [32, 4096, 1536], P('expert', 'dp', 'tensor'), may hold values from -0.09375 to 0.09375
- w_down: bfloat16 [32, 1536, 4096], P('expert', 'tensor', 'dp'), may hold values from -0.15625 to 0.15625
Outputs:
- grad_input: bfloat16 [4096, 4096], P('expert', ('dp', 'tensor'))
- grad_w_gate: bfloat16 [32, 4096, 1536], P('expert', 'dp', 'tensor')
- grad_w_up: bfloat16 [32, 4096, 1536], P('expert', 'dp', 'tensor')
- grad_w_down: bfloat16 [32, 1536, 4096], P('expert', 'tensor', 'dp')
The draws below stay inside these ranges and needn't reach their ends.
Inputs may be any that keep to these rules, and one draw needn't show every extreme that they name: `routes`: each row names 8 different experts. In the 128 rows of one device no expert is named by more than 40 rows, a bound that some block reaches.
All inputs are finite; a program needn't handle non-finite values.
Results may differ from the reference program's by a relative error of at most 0.025.
Values may be sent and summed in bfloat16 or wider, within the bound.
A program may use at most 64 MiB of HBM per device.

```python
import math
import jax
import jax.numpy as jnp
import numpy as np
from jax import lax

D = 4096
H = 1536
TOK = 128
EXPERTS = 32
TOPK = 8
CAP = 40
SLOTS = 1280
TOKENS = 4096
N_DP = 8
N_TENSOR = 4


def levels(stream_key, dims, shards, smallest, high):
    level = 1.0
    for dim, blocks in shards:
        steps = jax.random.uniform(jax.random.fold_in(jax.random.fold_in(stream_key, 6), dim), (blocks,), jnp.float32, smallest / len(shards), high / len(shards))
        level = level * jnp.repeat(jnp.exp(steps), dims[dim] // blocks).reshape((-1,) + (1,) * (len(dims) - 1 - dim))
    return level


def deal_out(key, own, number, rows, amount, top, bound, skew):
    ranking = jax.random.permutation(key, amount)
    packed, usual = load_shares(amount, rows * top, bound, skew, True), load_shares(amount, rows * top, bound, skew, False)
    places = jnp.arange(amount)

    def named(tallies, offset_by):
        used = int((tallies > 0).sum())
        fixed = max(1, used // 4)
        shifted = fixed + (places - fixed + offset_by * (used - fixed)) % max(1, amount - fixed)
        return jnp.zeros((amount,), jnp.int32).at[ranking[jnp.where(places < fixed, places, shifted)]].set(jnp.asarray(tallies, jnp.int32))

    tallies = jnp.where(number % 4 == 0, named(packed, number // 4), named(usual, number - number // 4 - 1))
    mixed = jax.random.permutation(jax.random.fold_in(own, 3), amount)
    donor, sink = mixed[0:amount // 2 * 2:2], mixed[1:amount // 2 * 2:2]
    room = jnp.minimum(tallies[donor] - 1, bound - tallies[sink]) // 2
    room = jnp.where((donor == ranking[0]) | (sink == ranking[0]) | (tallies[sink] == 0), 0, jnp.maximum(room, 0))
    shifted = jax.random.randint(jax.random.fold_in(own, 4), (amount // 2,), 0, 1 << 20) % (room + 1)
    tallies = tallies.at[donor].add(-shifted).at[sink].add(shifted)
    labels = jnp.searchsorted(jnp.cumsum(tallies), jnp.arange(rows * top), side="right").astype(jnp.int32)
    grid = labels.reshape(top, rows).T
    grid = grid[jax.random.permutation(jax.random.fold_in(own, 1), rows)]
    offset_by = jax.random.randint(jax.random.fold_in(own, 2), (rows, 1), 0, top)
    return jnp.take_along_axis(grid, (jnp.arange(top)[None, :] + offset_by) % top, axis=1)


def load_shares(count, total, bound, slope, full):
    portions = [(1 << 20) // math.isqrt(grade ** slope) + 1 for grade in range(1, count + 1)]
    largest = bound if full else min(bound, max(-(-total // count), total * portions[0] // sum(portions)))
    least = 1 if total - largest >= count - 1 else 0
    given, rest = [largest] + [least] * (count - 1), total - largest - least * (count - 1)
    while rest > 0:
        movable = [i for i in range(1, count) if given[i] < largest] or [i for i in range(1, count) if given[i] < bound]
        whole, remaining = sum([portions[i] for i in movable]), rest
        for i in movable:
            addition = min(bound - given[i], max(1, remaining * portions[i] // whole), rest)
            given[i] = given[i] + addition
            rest = rest - addition
    return np.array(given)


def noise(stream_key, extent, spread, most, shards=(), held_as=jnp.bfloat16):
    drawn = spread * jax.random.normal(stream_key, extent, jnp.float32)
    if shards:
        drawn = drawn * levels(stream_key, extent, shards, -0.22, 0.18)
    return jnp.clip(drawn, -most, most).astype(held_as)


def setup_inputs(seed: int = 0) -> dict:
    streams_of = jax.random.split(jax.random.key(seed), 10)
    grad_output = noise(streams_of[0], (TOKENS, D), 1.0, 6.0, ((0, 32), (1, 8)))
    gate_probs = jnp.clip(0.05 + 0.55 * jax.random.uniform(streams_of[1], (TOKENS, TOPK), jnp.float32) ** levels(streams_of[1], (TOKENS, TOPK), ((0, 32),), -0.2, 0.2), 0.05, 0.6)
    routes_keys = jax.random.split(jax.random.fold_in(streams_of[2], 1), TOKENS // TOK)
    routes_turns = jax.random.permutation(jax.random.fold_in(streams_of[2], 3), TOKENS // TOK)
    routes = jax.vmap(lambda own, number: deal_out(jax.random.fold_in(streams_of[2], 2), own, number, TOK, EXPERTS, TOPK, CAP, 2))(routes_keys, routes_turns).reshape((TOKENS, TOPK))
    saved_input = noise(streams_of[3], (EXPERTS, SLOTS, D), 1.0, 6.0, ((0, 32), (2, 8)))
    saved_gate = noise(streams_of[4], (EXPERTS, SLOTS, H), 1.5, 6.0, ((0, 32), (2, 4)))
    saved_up = noise(streams_of[5], (EXPERTS, SLOTS, H), 1.0, 6.0, ((0, 32), (2, 4)))
    w_gate = noise(streams_of[6], (EXPERTS, D, H), D ** -0.5, 0.09375, ((0, 32), (1, 8), (2, 4)))
    w_up = noise(streams_of[7], (EXPERTS, D, H), D ** -0.5, 0.09375, ((0, 32), (1, 8), (2, 4)))
    w_down = noise(streams_of[8], (EXPERTS, H, D), H ** -0.5, 0.15625, ((0, 32), (1, 4), (2, 8)))
    return {"grad_output": grad_output, "gate_probs": gate_probs, "routes": routes, "saved_input": saved_input, "saved_gate": saved_gate, "saved_up": saved_up, "w_gate": w_gate, "w_up": w_up, "w_down": w_down}


def reference(grad_output, gate_probs, routes, saved_input, saved_gate, saved_up, w_gate, w_up, w_down):
    count = TOKENS * TOPK
    flat = routes.reshape(-1).astype(jnp.int32)
    positions = jnp.arange(count, dtype=jnp.int32)
    onehot = (flat[:, None] == jnp.arange(EXPERTS, dtype=jnp.int32)[None, :]).astype(jnp.int32)
    onehot = onehot.reshape(EXPERTS, TOK * TOPK, EXPERTS)
    ranks = jnp.sum((jnp.cumsum(onehot, axis=1) - onehot) * onehot, axis=2).reshape(-1)
    slot = (positions // (TOK * TOPK)) * CAP + ranks
    target = flat * SLOTS + slot
    source = jnp.zeros((EXPERTS * SLOTS,), jnp.int32).at[target].set(positions).reshape(EXPERTS, SLOTS)
    valid = jnp.zeros((EXPERTS * SLOTS,), jnp.float32).at[target].set(1.0).reshape(EXPERTS, SLOTS)
    probs_flat = gate_probs.reshape(-1)
    width_block = D // N_DP
    hidden_block = H // N_TENSOR

    def one_expert(total, expert_id):
        where = source[expert_id]
        live = valid[expert_id]
        owner = where // TOPK
        rows = (grad_output[owner].astype(jnp.float32) * (probs_flat[where] * live)[:, None]).astype(jnp.bfloat16)
        rows_f = rows.astype(jnp.float32)
        down_f = w_down[expert_id].astype(jnp.float32)
        parts = jnp.einsum('snd,hnd->nsh', rows_f.reshape(SLOTS, N_DP, width_block), down_f.reshape(H, N_DP, width_block))
        grad_hidden = jnp.sum(parts.astype(jnp.bfloat16).astype(jnp.float32), axis=0)
        gate = saved_gate[expert_id].astype(jnp.float32)
        upper = saved_up[expert_id].astype(jnp.float32)
        sig = jax.nn.sigmoid(gate)
        act = gate * sig
        hidden = (act * upper).astype(jnp.bfloat16)
        grad_up_rows = (grad_hidden * act).astype(jnp.bfloat16)
        grad_gate_rows = (grad_hidden * upper * sig * (1.0 + gate * (1.0 - sig))).astype(jnp.bfloat16)
        grad_down = jnp.einsum('sh,sd->hd', hidden.astype(jnp.float32), rows_f).astype(jnp.bfloat16)
        inputs_f = saved_input[expert_id].astype(jnp.float32)
        gg_f = grad_gate_rows.astype(jnp.float32)
        gu_f = grad_up_rows.astype(jnp.float32)
        grad_gate = jnp.einsum('sd,sh->dh', inputs_f, gg_f).astype(jnp.bfloat16)
        grad_up = jnp.einsum('sd,sh->dh', inputs_f, gu_f).astype(jnp.bfloat16)
        wg_f = w_gate[expert_id].astype(jnp.float32).reshape(D, N_TENSOR, hidden_block)
        wu_f = w_up[expert_id].astype(jnp.float32).reshape(D, N_TENSOR, hidden_block)
        pieces = jnp.einsum('snh,dnh->nsd', gg_f.reshape(SLOTS, N_TENSOR, hidden_block), wg_f)
        pieces = pieces + jnp.einsum('snh,dnh->nsd', gu_f.reshape(SLOTS, N_TENSOR, hidden_block), wu_f)
        back = jnp.sum(pieces.astype(jnp.bfloat16).astype(jnp.float32), axis=0) * live[:, None]
        total = total.at[owner].add(back)
        return total, (grad_gate, grad_up, grad_down)

    total, grads = lax.scan(one_expert, jnp.zeros((TOKENS, D), jnp.float32), jnp.arange(EXPERTS, dtype=jnp.int32))
    return (total.astype(jnp.bfloat16), grads[0], grads[1], grads[2])
```

```python
import functools

import jax
import jax.numpy as jnp
from jax import lax
from jax.experimental import pallas as pl
from jax.experimental.pallas import tpu as pltpu
from jax.sharding import PartitionSpec as P

X = 4
Y = 8
CAP = 40
ROWS = Y * CAP
PIECES = 4
PIECE = ROWS // PIECES
BF16 = jnp.bfloat16
F32 = jnp.float32
SLACK = 2


def mod(a, n):
    return lax.rem(a + 2 * n, n)


def turn(k):
    return jnp.where(k == 2, 3, jnp.where(k == 3, 2, k))


def dot(a, b, dims):
    return lax.dot_general(a, b, (dims, ((), ())), preferred_element_type=F32)


def kernel(
    routes, probs, go, sin_h, sg_h, su_h, wg_h, wu_h, wd_h,
    gi, gwg_h, gwu_h, gwd_h,
    sin, sg, su, wg, wu, wd,
    meta, gbuf, sel, stage, xsend, arr, part, inb, tot, gg, gu, hid, pr, crecv, rsend, rret,
    ys, yr, zs, zr, acc, grad,
    load_sem, out_sem,
    ms, mr, gs, gr, xs_sem, xr_sem, cs, cr, ps, prs, ts, tr, ds, dr, qs, qr, yss, yrs, zss, zrs,
):
    dp = lax.axis_index("dp")
    e = lax.axis_index("expert")
    t = lax.axis_index("tensor")
    x, y = e // Y, lax.rem(e, Y)
    h, c = t // 2, lax.rem(t, 2)
    n_dp = 8
    low = dp < n_dp // 2
    pos = jnp.where(low, dp, n_dp - 1 - dp)
    inward = jnp.where(low, dp + 1, dp - 1)
    outward = jnp.where(low, dp - 1, dp + 1)
    mid = n_dp // 2 - 1

    y_next = {"expert": x * Y + mod(y + 1, Y)}
    y_prev = {"expert": x * Y + mod(y - 1, Y)}
    x_at = lambda xx: {"expert": xx * Y + y}
    other_core = {"tensor": h * 2 + 1 - c}
    other_z = {"tensor": (1 - h) * 2 + c}
    at_in = {"dp": inward}
    at_out = {"dp": outward}

    barrier = pltpu.get_barrier_semaphore()

    def greet(where):
        pl.semaphore_signal(barrier, inc=1, device_id=where, device_id_type=pl.DeviceIdType.MESH)

    for where in (y_next, y_prev, other_core, other_z, at_in):
        greet(where)
    for off in (1, 2, 3):
        greet(x_at(mod(x + off, X)))

    @pl.when(pos > 0)
    def _():
        greet(at_out)

    def remote(src, dst, ssem, rsem, where):
        return pltpu.make_async_remote_copy(
            src_ref=src, dst_ref=dst, send_sem=ssem, recv_sem=rsem,
            device_id=where, device_id_type=pl.DeviceIdType.MESH,
        )

    half = gbuf.shape[2]
    loads = [
        pltpu.make_async_copy(go.at[:, pl.ds(pl.multiple_of(c * half, half), half)], gbuf.at[y], load_sem.at[0])
    ]
    for i, (src, dst) in enumerate(((wd_h, wd), (sg_h, sg), (su_h, su), (wg_h, wg), (wu_h, wu), (sin_h, sin))):
        loads.append(pltpu.make_async_copy(src, dst, load_sem.at[i + 1]))
    for copy in loads:
        copy.start()

    meta[y, 0:8, :] = routes[...].astype(F32)
    meta[y, 8:16, :] = probs[...]
    tokens = routes.shape[1]
    upper = (
        lax.broadcasted_iota(jnp.int32, (tokens, tokens), 0)
        < lax.broadcasted_iota(jnp.int32, (tokens, tokens), 1)
    ).astype(F32)
    names = (lax.broadcasted_iota(jnp.int32, (8, tokens), 0) * Y + y).astype(F32)
    ranks_of = lax.broadcasted_iota(jnp.int32, (CAP, tokens), 0).astype(F32)

    loads[0].wait()
    pl.semaphore_wait(barrier, jnp.where(pos > 0, 9, 8))

    def ring(buf, ssem, rsem, k, way):
        block = mod(y - (k - 1) * way, Y)
        slot = (k - 1) if way > 0 else (Y // 2 + k - 1)
        return remote(
            buf.at[block], buf.at[block], ssem.at[slot], rsem.at[block],
            y_next if way > 0 else y_prev,
        )

    def ring_arrived(k, way):
        block = mod(y - k * way, Y)
        remote(meta.at[block], meta.at[block], ms.at[0], mr.at[block], y_next).wait_recv()
        remote(gbuf.at[block], gbuf.at[block], gs.at[0], gr.at[block], y_next).wait_recv()
        return block

    def ring_send(k, way):
        ring(meta, ms, mr, k, way).start()
        ring(gbuf, gs, gr, k, way).start()

    def choose(block):
        named = meta[block, 0:8, :]
        weights = meta[block, 8:16, :]
        hits = jnp.zeros((8, tokens), F32)
        weight = jnp.zeros((8, tokens), F32)
        for k in range(8):
            same = named[k : k + 1, :] == names
            hits = hits + jnp.where(same, 1.0, 0.0)
            weight = weight + jnp.where(same, weights[k : k + 1, :], 0.0)
        rank = dot(hits, upper, ((1,), (0,)))
        rank = jnp.where(hits > 0.0, rank, -1.0)
        masks, scales = [], []
        for i in range(X):
            mask = jnp.where(rank[i : i + 1, :] == ranks_of, 1.0, 0.0)
            masks.append(mask)
            scales.append(jnp.sum(mask * weight[i : i + 1, :], axis=1, keepdims=True))
        mask = jnp.concatenate(masks, axis=0)
        sel[block] = mask
        rows = dot(mask.astype(BF16), gbuf[block], ((1,), (0,))) * jnp.concatenate(scales, axis=0)
        at = pl.ds(pl.multiple_of(block * CAP, 8), CAP)
        for i in range(X):
            stage[i, at, :] = rows[i * CAP : (i + 1) * CAP, :]

    ring_send(1, 1)
    ring_send(1, -1)
    choose(y)
    for k in range(1, Y // 2 + 1):
        right = ring_arrived(k, 1)
        if k < Y // 2:
            ring_send(k + 1, 1)
            left = ring_arrived(k, -1)
            if k < Y // 2 - 1:
                ring_send(k + 1, -1)
            choose(right)
            choose(left)
        else:
            choose(right)

    def core_pass(xx):
        return remote(arr.at[c, xx], arr.at[c, xx], cs.at[xx], cr.at[xx], other_core)

    def core_arrival(xx):
        return remote(arr.at[1 - c, xx], arr.at[1 - c, xx], cs.at[xx], cr.at[xx], other_core)

    def x_pass(off):
        to = mod(x + off, X)
        return remote(xsend.at[to], arr.at[c, x], xs_sem.at[off - 1], xr_sem.at[x], x_at(to))

    def x_arrival(xx):
        return remote(xsend.at[xx], arr.at[c, xx], xs_sem.at[0], xr_sem.at[xx], x_at(xx))

    arr[c, x] = stage[x].astype(BF16)
    core_pass(x).start()
    for off in (1, 3, 2):
        to = mod(x + off, X)
        xsend[to] = stage[to].astype(BF16)
        x_pass(off).start()
    for copy in loads[1:]:
        copy.wait()

    def add_in(ch):
        return remote(part.at[ch], inb.at[ch], ps.at[ch], prs.at[ch], at_in)

    def add_mid(ch):
        return remote(part.at[ch], tot.at[ch], ps.at[ch], tr.at[ch], at_in)

    def total_out(ch):
        return remote(tot.at[ch], tot.at[ch], ts.at[ch], tr.at[ch], at_out)

    def core_sum(xx):
        return remote(pr.at[xx, 1 - c], crecv.at[xx], ds.at[xx], dr.at[xx], other_core)

    def x_return(xx, off_slot):
        return remote(rsend.at[xx], rret.at[x], qs.at[off_slot], qr.at[x], x_at(xx))

    def x_returned(xx):
        return remote(rsend.at[xx], rret.at[xx], qs.at[xx], qr.at[xx], x_at(xx))

    count = X * PIECES
    lag = SLACK * (2 * (mid - pos) + 1)

    def step(s, carry):
        @pl.when(s < count)
        def _():
            k, q = s // PIECES, lax.rem(s, PIECES)
            xx = mod(x + turn(k), X)
            ch = xx * PIECES + q

            @pl.when(q == 0)
            def _():
                core_arrival(xx).wait_recv()
                partial = dot(arr[0, xx], wd[:, :half], ((1,), (1,)))
                partial = partial + dot(arr[1, xx], wd[:, half:], ((1,), (1,)))
                for i in range(PIECES):
                    part[xx * PIECES + i] = partial[i * PIECE : (i + 1) * PIECE, :].astype(BF16)

            @pl.when(pos > 0)
            def _():
                add_in(ch).wait_recv()
                part[ch] = (part[ch].astype(F32) + inb[ch].astype(F32)).astype(BF16)

            @pl.when(pos < mid)
            def _():
                add_in(ch).start()

            @pl.when(pos == mid)
            def _():
                add_mid(ch).start()

            @pl.when((q == 2) & (k < X - 1))
            def _():
                xn = mod(x + turn(k + 1), X)
                x_arrival(xn).wait_recv()
                core_pass(xn).start()

        u = s - lag

        @pl.when((u >= 0) & (u < count))
        def _():
            k, q = u // PIECES, lax.rem(u + PIECES, PIECES)
            xx = mod(x + turn(k), X)
            ch = xx * PIECES + q
            total_out(ch).wait_recv()

            @pl.when(pos == mid)
            def _():
                tot[ch] = (part[ch].astype(F32) + tot[ch].astype(F32)).astype(BF16)

            @pl.when(pos > 0)
            def _():
                total_out(ch).start()

            gate = sg[ch].astype(F32)
            upper_ = su[ch].astype(F32)
            sig = jax.nn.sigmoid(gate)
            act = gate * sig
            grad_hidden = tot[ch].astype(F32)
            hid[ch] = (act * upper_).astype(BF16)
            gu[ch] = (grad_hidden * act).astype(BF16)
            gg[ch] = (grad_hidden * upper_ * sig * (1.0 + gate * (1.0 - sig))).astype(BF16)

            @pl.when(q == PIECES - 1)
            def _():
                at = pl.ds(xx * PIECES, PIECES)
                width = gg.shape[2]
                g1 = gg[at].reshape(ROWS, width)
                g2 = gu[at].reshape(ROWS, width)
                rows = dot(g1, wg[...], ((1,), (1,))) + dot(g2, wu[...], ((1,), (1,)))
                quarter = rows.shape[1] // 4
                for i in range(4):
                    pr[xx, i % 2, i // 2] = rows[:, i * quarter : (i + 1) * quarter].astype(BF16)
                core_sum(xx).start()

        v = u - 5

        @pl.when((v >= 0) & (lax.rem(v + PIECES * 64, PIECES) == 0))
        def _():
            k = v // PIECES
            xx = mod(x + turn(k), X)
            core_sum(xx).wait_recv()
            both = (pr[xx, c].astype(F32) + crecv[xx].astype(F32)).astype(BF16)

            @pl.when(xx == x)
            def _():
                rret[x] = both

            @pl.when(xx != x)
            def _():
                rsend[xx] = both
                x_return(xx, xx).start()

        return carry

    lax.fori_loop(0, count + 2 + lag, step, 0)

    width = gg.shape[2]

    def weight_grad(left, right, slot, result, transposed):
        def body(xx, carry):
            at = pl.ds(xx * PIECES, PIECES)
            if transposed:
                a = left[at].reshape(ROWS, width)
                for i in range(2):
                    cut = slice(i * half, (i + 1) * half)
                    term = dot(a, arr[i, xx], ((0,), (0,)))
                    acc_d[:, cut] = jnp.where(xx == 0, term, acc_d[:, cut] + term)
            else:
                term = dot(left[xx], right[at].reshape(ROWS, width), ((0,), (0,)))
                acc_g[...] = jnp.where(xx == 0, term, acc_g[...] + term)
            return carry

        acc_d = acc.at[pl.ds(0, width), :]
        acc_g = acc.at[:, pl.ds(0, width)]
        lax.fori_loop(0, X, body, 0)
        if transposed:
            grad[slot, pl.ds(0, width), :] = acc_d[...].astype(BF16)
            src = grad.at[slot, pl.ds(0, width), :]
        else:
            grad[slot, :, pl.ds(0, width)] = acc_g[...].astype(BF16)
            src = grad.at[slot, :, pl.ds(0, width)]
        copy = pltpu.make_async_copy(src, result, out_sem.at[slot])
        copy.start()
        return copy

    outs = [weight_grad(hid, None, 0, gwd_h, True)]

    for off in (1, 2, 3):
        x_returned(mod(x + off, X)).wait_recv()
    quarter = rret.shape[3]
    for i in range(X):
        for j in range(2):
            stage[i, :, j * quarter : (j + 1) * quarter] = rret[i, j].astype(F32)

    def combine(block):
        at = pl.ds(pl.multiple_of(block * CAP, 8), CAP)
        rows = jnp.concatenate([stage[i, at, :] for i in range(X)], axis=0)
        return dot(sel[block], rows, ((0,), (0,)))

    def y_copy(slot, way):
        return remote(ys.at[slot], yr.at[slot], yss.at[slot], yrs.at[slot], y_next if way > 0 else y_prev)

    turns = Y // 2
    for k in range(1, turns + 1):
        val = combine(mod(y + turns + 1 - k, Y))
        if k > 1:
            y_copy(k - 2, 1).wait_recv()
            val = val + yr[k - 2].astype(F32)
        ys[k - 1] = val.astype(BF16)
        y_copy(k - 1, 1).start()
        if k < turns:
            val = combine(mod(y - turns + k, Y))
            if k > 1:
                y_copy(turns + k - 2, -1).wait_recv()
                val = val + yr[turns + k - 2].astype(F32)
            ys[turns + k - 1] = val.astype(BF16)
            y_copy(turns + k - 1, -1).start()
        if k == 1:
            outs.append(weight_grad(sin, gg, 1, gwg_h, False))
        if k == 2:
            outs.append(weight_grad(sin, gu, 2, gwu_h, False))
    val = combine(y)
    y_copy(turns - 1, 1).wait_recv()
    y_copy(2 * turns - 2, -1).wait_recv()
    val = val + yr[turns - 1].astype(F32) + yr[2 * turns - 2].astype(F32)

    first = h == 0
    zs[...] = jnp.where(first, val[:, quarter:], val[:, :quarter]).astype(BF16)
    last = remote(zs, zr, zss, zrs, other_z)
    last.start()
    keep = jnp.where(first, val[:, :quarter], val[:, quarter:])
    last.wait_recv()
    gi[...] = (keep + zr[...].astype(F32)).astype(BF16)

    for k in range(1, Y // 2 + 1):
        for way in (1, -1):
            if way > 0 or k < Y // 2:
                ring(meta, ms, mr, k, way).wait_send()
                ring(gbuf, gs, gr, k, way).wait_send()
                y_copy(k - 1 if way > 0 else turns + k - 1, way).wait_send()
    for off in (1, 2, 3):
        x_pass(off).wait_send()
        to = mod(x + off, X)
        x_return(to, to).wait_send()
    for i in range(X):
        core_pass(i).wait_send()
        core_sum(i).wait_send()

    def sent(ch, carry):
        add_in(ch).wait_send()

        @pl.when(pos > 0)
        def _():
            total_out(ch).wait_send()

        return carry

    lax.fori_loop(0, count, sent, 0)
    last.wait_send()
    for copy in outs:
        copy.wait()


def per_device(
    grad_output, gate_probs, routes, saved_input, saved_gate, saved_up, w_gate, w_up, w_down
):
    tokens, width = grad_output.shape
    hidden = saved_gate.shape[2]
    count = X * PIECES
    half, quarter = width // 2, width // 4
    dma = lambda *n: pltpu.SemaphoreType.DMA(n)
    vmem = pl.BlockSpec(memory_space=pltpu.VMEM)
    hbm = pl.BlockSpec(memory_space=pl.ANY)
    piece = (count, PIECE, hidden)
    outs = pl.pallas_call(
        kernel,
        out_shape=(
            jax.ShapeDtypeStruct((tokens, quarter), BF16),
            jax.ShapeDtypeStruct((width, hidden), BF16),
            jax.ShapeDtypeStruct((width, hidden), BF16),
            jax.ShapeDtypeStruct((hidden, width), BF16),
        ),
        in_specs=[vmem] * 2 + [hbm] * 7,
        out_specs=(vmem, hbm, hbm, hbm),
        scratch_shapes=[
            pltpu.VMEM((X, ROWS, width), BF16),
            pltpu.VMEM(piece, BF16),
            pltpu.VMEM(piece, BF16),
            pltpu.VMEM((width, hidden), BF16),
            pltpu.VMEM((width, hidden), BF16),
            pltpu.VMEM((hidden, width), BF16),
            pltpu.VMEM((Y, 16, tokens), F32),
            pltpu.VMEM((Y, tokens, half), BF16),
            pltpu.VMEM((Y, X * CAP, tokens), F32),
            pltpu.VMEM((X, ROWS, half), F32),
            pltpu.VMEM((X, ROWS, half), BF16),
            pltpu.VMEM((2, X, ROWS, half), BF16),
            pltpu.VMEM(piece, BF16),
            pltpu.VMEM(piece, BF16),
            pltpu.VMEM(piece, BF16),
            pltpu.VMEM(piece, BF16),
            pltpu.VMEM(piece, BF16),
            pltpu.VMEM(piece, BF16),
            pltpu.VMEM((X, 2, 2, ROWS, quarter), BF16),
            pltpu.VMEM((X, 2, ROWS, quarter), BF16),
            pltpu.VMEM((X, 2, ROWS, quarter), BF16),
            pltpu.VMEM((X, 2, ROWS, quarter), BF16),
            pltpu.VMEM((Y, tokens, half), BF16),
            pltpu.VMEM((Y, tokens, half), BF16),
            pltpu.VMEM((tokens, quarter), BF16),
            pltpu.VMEM((tokens, quarter), BF16),
            pltpu.VMEM((width, width), F32),
            pltpu.VMEM((3, width, width), BF16),
            dma(7), dma(3),
            dma(Y), dma(Y), dma(Y), dma(Y),
            dma(X), dma(X), dma(X), dma(X),
            dma(count), dma(count), dma(count), dma(count),
            dma(X), dma(X), dma(X), dma(X),
            dma(Y), dma(Y), pltpu.SemaphoreType.DMA, pltpu.SemaphoreType.DMA,
        ],
        compiler_params=pltpu.CompilerParams(
            collective_id=0, has_side_effects=True, vmem_limit_bytes=56 * 1024 * 1024
        ),
        cost_estimate=pl.CostEstimate(
            flops=10 * X * ROWS * width * hidden, bytes_accessed=6_000_000, transcendentals=X * ROWS * hidden
        ),
    )(
        routes.T, gate_probs.T, grad_output,
        saved_input.reshape(X, ROWS, width),
        saved_gate.reshape(piece), saved_up.reshape(piece),
        w_gate[0], w_up[0], w_down[0],
    )
    return outs[0], outs[1][None], outs[2][None], outs[3][None]


def solution(mesh):
    placed = (
        P("expert", "dp"),
        P("expert", None),
        P("expert", None),
        P("expert", None, "dp"),
        P("expert", None, "tensor"),
        P("expert", None, "tensor"),
        P("expert", "dp", "tensor"),
        P("expert", "dp", "tensor"),
        P("expert", "tensor", "dp"),
    )
    return jax.shard_map(
        per_device,
        mesh=mesh,
        in_specs=placed,
        out_specs=(
            P("expert", ("dp", "tensor")),
            P("expert", "dp", "tensor"),
            P("expert", "dp", "tensor"),
            P("expert", "tensor", "dp"),
        ),
        check_vma=False,
    )
```

```python
import jax
import jax.numpy as jnp
from jax import lax
from jax.experimental import pallas as pl
from jax.experimental.pallas import tpu as pltpu
from jax.sharding import PartitionSpec as P

X = 4
Y = 8
CAP = 40
ROWS = Y * CAP
BLOCK = X * CAP
PIECES = 2
PIECE = BLOCK // PIECES
BF16 = jnp.bfloat16
F32 = jnp.float32
SLACK = 3


def mod(a, n):
    return lax.rem(a + 2 * n, n)


def turn(k):
    far = Y // 2 - k // 2
    return jnp.where(k == 0, 0, jnp.where((lax.rem(k, 2) == 1) & (k > 1), -far, far))


def dot(a, b, dims):
    return lax.dot_general(a, b, (dims, ((), ())), preferred_element_type=F32)


def kernel(
    routes, probs, go, sin_h, sg_h, su_h, wg_h, wu_h, wd_h,
    gi, gwg_h, gwu_h, gwd_h,
    sin, sg, su, wg, wu, wd,
    meta, gbuf, sel, selt, stage, ysend, arr, part, inb, tot, a1, a2, hid, gg, gu,
    pr, crecv, rsend, rret, xo, xi, zs, zr, acc, grad,
    load_sem, out_sem,
    ms, mr, gs, gr, ys_sem, yr_sem, cs, cr, ps, prs, ts, tr, ds, dr, qs, qr, xos, xis, zss, zrs,
):
    dp = lax.axis_index("dp")
    e = lax.axis_index("expert")
    t = lax.axis_index("tensor")
    x, y = e // Y, lax.rem(e, Y)
    h, c = t // 2, lax.rem(t, 2)
    n_dp = 8
    low = dp < n_dp // 2
    pos = jnp.where(low, dp, n_dp - 1 - dp)
    inward = jnp.where(low, dp + 1, dp - 1)
    outward = jnp.where(low, dp - 1, dp + 1)
    mid = n_dp // 2 - 1

    x_at = lambda xx: {"expert": xx * Y + y}
    y_at = lambda yy: {"expert": x * Y + yy}
    other_core = {"tensor": h * 2 + 1 - c}
    other_z = {"tensor": (1 - h) * 2 + c}
    at_in = {"dp": inward}
    at_out = {"dp": outward}

    barrier = pltpu.get_barrier_semaphore()

    def greet(where):
        pl.semaphore_signal(barrier, inc=1, device_id=where, device_id_type=pl.DeviceIdType.MESH)

    for off in (1, 2, 3):
        greet(x_at(mod(x + off, X)))
    for off in range(1, Y):
        greet(y_at(mod(y + off, Y)))
    for where in (other_core, other_z, at_in):
        greet(where)

    @pl.when(pos > 0)
    def _():
        greet(at_out)

    def remote(src, dst, ssem, rsem, where):
        return pltpu.make_async_remote_copy(
            src_ref=src, dst_ref=dst, send_sem=ssem, recv_sem=rsem,
            device_id=where, device_id_type=pl.DeviceIdType.MESH,
        )

    half = gbuf.shape[2]
    loads = [
        pltpu.make_async_copy(go.at[:, pl.ds(pl.multiple_of(c * half, half), half)], gbuf.at[x], load_sem.at[0])
    ]
    for i, (src, dst) in enumerate(((sg_h, sg), (su_h, su), (wd_h, wd), (wg_h, wg), (wu_h, wu), (sin_h, sin))):
        loads.append(pltpu.make_async_copy(src, dst, load_sem.at[i + 1]))
    for copy in loads:
        copy.start()

    meta[x, 0:8, :] = routes[...].astype(F32)
    meta[x, 8:16, :] = probs[...]
    tokens = routes.shape[1]
    loads[0].wait()
    pl.semaphore_wait(barrier, jnp.where(pos > 0, Y - 1 + 7, Y - 1 + 6))

    def x_meta(off, at):
        return remote(meta.at[at], meta.at[at], ms.at[off], mr.at[at], x_at(mod(x + off, X)))

    def x_rows(off, at):
        return remote(gbuf.at[at], gbuf.at[at], gs.at[off], gr.at[at], x_at(mod(x + off, X)))

    for off in (1, 3, 2):
        x_meta(off, x).start()
        x_rows(off, x).start()

    upper = (
        lax.broadcasted_iota(jnp.int32, (tokens, tokens), 0)
        < lax.broadcasted_iota(jnp.int32, (tokens, tokens), 1)
    ).astype(F32)
    names = (lax.broadcasted_iota(jnp.int32, (Y, tokens), 0) + x * Y).astype(F32)
    ranks_of = lax.broadcasted_iota(jnp.int32, (CAP, tokens), 0).astype(F32)

    def choose(block):
        named = meta[block, 0:8, :]
        weights = meta[block, 8:16, :]
        hits = jnp.zeros((Y, tokens), F32)
        weight = jnp.zeros((Y, tokens), F32)
        for k in range(8):
            same = named[k : k + 1, :] == names
            hits = hits + jnp.where(same, 1.0, 0.0)
            weight = weight + jnp.where(same, weights[k : k + 1, :], 0.0)
        rank = dot(hits, upper, ((1,), (0,)))
        rank = jnp.where(hits > 0.0, rank, -1.0)
        masks, scales = [], []
        for i in range(Y):
            mask = jnp.where(rank[i : i + 1, :] == ranks_of, 1.0, 0.0)
            masks.append(mask)
            scales.append(jnp.sum(mask * weight[i : i + 1, :], axis=1, keepdims=True))
        mask = jnp.concatenate(masks, axis=0)
        sel[block] = mask
        rows = dot(mask.astype(BF16), gbuf[block], ((1,), (0,))) * jnp.concatenate(scales, axis=0)
        at = pl.ds(pl.multiple_of(block * CAP, 8), CAP)
        for i in range(Y):
            stage[i, at, :] = rows[i * CAP : (i + 1) * CAP, :]

    choose(x)

    loads[1].wait()
    loads[2].wait()

    def activate(i, carry):
        gates = sg[i].astype(F32)
        ups = su[i].astype(F32)
        at = pl.ds(pl.multiple_of(i * CAP, 8), CAP)
        for yy in range(Y):
            gate = gates[yy * CAP : (yy + 1) * CAP, :]
            up = ups[yy * CAP : (yy + 1) * CAP, :]
            sig = jax.nn.sigmoid(gate)
            act = gate * sig
            a1[yy, at, :] = act
            a2[yy, at, :] = up * sig * (1.0 + gate * (1.0 - sig))
            hid[yy, at, :] = act * up
        return carry

    lax.fori_loop(0, X, activate, 0)

    for off in (1, 3, 2):
        xx = mod(x + off, X)
        x_meta(off, xx).wait_recv()
        x_rows(off, xx).wait_recv()
        choose(xx)

    def core_pass(yy):
        return remote(arr.at[c, yy], arr.at[c, yy], cs.at[yy], cr.at[yy], other_core)

    def core_arrival(yy):
        return remote(arr.at[1 - c, yy], arr.at[1 - c, yy], cs.at[yy], cr.at[yy], other_core)

    def y_pass(to):
        return remote(ysend.at[to], arr.at[c, y], ys_sem.at[to], yr_sem.at[y], y_at(to))

    def y_arrival(yy):
        return remote(ysend.at[yy], arr.at[c, yy], ys_sem.at[yy], yr_sem.at[yy], y_at(yy))

    arr[c, y] = stage[y].astype(BF16)
    core_pass(y).start()
    for off in (4, 3, -3, 2, -2, 1, -1):
        to = mod(y + off, Y)
        ysend[to] = stage[to].astype(BF16)
        y_pass(to).start()
    for copy in loads[3:]:
        copy.wait()

    def add_in(ch):
        return remote(part.at[ch], inb.at[ch], ps.at[ch], prs.at[ch], at_in)

    def add_mid(ch):
        return remote(part.at[ch], tot.at[ch], ps.at[ch], tr.at[ch], at_in)

    def total_out(ch):
        return remote(tot.at[ch], tot.at[ch], ts.at[ch], tr.at[ch], at_out)

    def core_sum(yy):
        return remote(pr.at[yy, 1 - c], crecv.at[yy], ds.at[yy], dr.at[yy], other_core)

    def y_return(yy):
        return remote(rsend.at[yy], rret.at[y], qs.at[yy], qr.at[y], y_at(yy))

    def y_returned(yy):
        return remote(rsend.at[yy], rret.at[yy], qs.at[yy], qr.at[yy], y_at(yy))

    count = Y * PIECES
    lag = SLACK * (2 * (mid - pos) + 1)
    width = wd.shape[0]

    def save(slot, value, result):
        rows, columns = value.shape
        where = grad.at[slot, pl.ds(0, rows), pl.ds(0, columns)]
        where[...] = value.astype(BF16)
        return pltpu.make_async_copy(where, result, out_sem.at[slot])

    def down_grad():
        part_acc = acc.at[pl.ds(0, width), :]

        def body(yy, carry):
            a = hid[yy].astype(BF16)
            for i in range(2):
                cut = slice(i * half, (i + 1) * half)
                term = dot(a, arr[i, yy], ((0,), (0,)))
                part_acc[:, cut] = jnp.where(yy == 0, term, part_acc[:, cut] + term)
            return carry

        lax.fori_loop(0, Y, body, 0)
        save(0, part_acc[...], gwd_h).start()

    def step(s, carry):
        @pl.when(s < count)
        def _():
            k, q = s // PIECES, lax.rem(s, PIECES)
            yy = mod(y + turn(k), Y)
            ch = yy * PIECES + q

            @pl.when(q == 0)
            def _():
                core_arrival(yy).wait_recv()
                partial = dot(arr[0, yy], wd[:, :half], ((1,), (1,)))
                partial = partial + dot(arr[1, yy], wd[:, half:], ((1,), (1,)))
                for i in range(PIECES):
                    part[yy * PIECES + i] = partial[i * PIECE : (i + 1) * PIECE, :].astype(BF16)

            @pl.when(pos > 0)
            def _():
                add_in(ch).wait_recv()
                part[ch] = (part[ch].astype(F32) + inb[ch].astype(F32)).astype(BF16)

            @pl.when(pos < mid)
            def _():
                add_in(ch).start()

            @pl.when(pos == mid)
            def _():
                add_mid(ch).start()

            @pl.when((s >= 1) & (s < Y))
            def _():
                yn = mod(y + turn(s), Y)
                y_arrival(yn).wait_recv()
                core_pass(yn).start()

        @pl.when(s == count)
        def _():
            down_grad()

        u = s - lag

        @pl.when((u >= 0) & (u < count))
        def _():
            k, q = u // PIECES, lax.rem(u + PIECES, PIECES)
            yy = mod(y + turn(k), Y)
            ch = yy * PIECES + q
            total_out(ch).wait_recv()

            @pl.when(pos == mid)
            def _():
                tot[ch] = (part[ch].astype(F32) + tot[ch].astype(F32)).astype(BF16)

            @pl.when(pos > 0)
            def _():
                total_out(ch).start()

            at = pl.ds(pl.multiple_of(q * PIECE, 8), PIECE)
            grad_hidden = tot[ch].astype(F32)
            gu[yy, at, :] = (grad_hidden * a1[yy, at, :]).astype(BF16).astype(F32)
            gg[yy, at, :] = (grad_hidden * a2[yy, at, :]).astype(BF16).astype(F32)

            @pl.when(q == PIECES - 1)
            def _():
                rows = dot(gg[yy].astype(BF16), wg[...], ((1,), (1,)))
                rows = rows + dot(gu[yy].astype(BF16), wu[...], ((1,), (1,)))
                quarter = rows.shape[1] // 4
                for i in range(4):
                    pr[yy, i % 2, i // 2] = rows[:, i * quarter : (i + 1) * quarter].astype(BF16)
                core_sum(yy).start()

        v = u - PIECES - 1

        @pl.when((v >= 0) & (lax.rem(v + PIECES * 64, PIECES) == 0))
        def _():
            yy = mod(y + turn(v // PIECES), Y)
            core_sum(yy).wait_recv()
            both = (pr[yy, c].astype(F32) + crecv[yy].astype(F32)).astype(BF16)

            @pl.when(yy == y)
            def _():
                rret[y] = both

            @pl.when(yy != y)
            def _():
                rsend[yy] = both
                y_return(yy).start()

        return carry

    lax.fori_loop(0, count + 2 + lag, step, 0)

    def weight_grad(rows, slot, result):
        whole = acc.at[:, pl.ds(0, width)]

        def body(i, carry):
            at = pl.ds(pl.multiple_of(i * CAP, 8), CAP)
            b = jnp.concatenate([rows[yy, at, :] for yy in range(Y)], axis=0).astype(BF16)
            term = dot(sin[i], b, ((0,), (0,)))
            whole[...] = jnp.where(i == 0, term, whole[...] + term)
            return carry

        lax.fori_loop(0, X, body, 0)
        copy = save(slot, whole[...], result)
        copy.start()
        return copy

    for i in range(X):
        selt[i] = sel[i].T
    outs = [weight_grad(gg, 1, gwg_h)]

    quarter = rret.shape[3]
    for i in range(Y):
        yy = mod(y + turn(i), Y)

        @pl.when(yy != y)
        def _():
            y_returned(yy).wait_recv()

        for j in range(2):
            stage[yy, :, j * quarter : (j + 1) * quarter] = rret[yy, j].astype(F32)

    def combine(block):
        at = pl.ds(pl.multiple_of(block * CAP, 8), CAP)
        rows = jnp.concatenate([stage[i, at, :] for i in range(Y)], axis=0)
        return dot(selt[block], rows, ((1,), (0,)))

    def x_sum(to):
        return remote(xo.at[to], xi.at[x], xos.at[to], xis.at[x], x_at(to))

    def x_summed(frm):
        return remote(xo.at[frm], xi.at[frm], xos.at[frm], xis.at[frm], x_at(frm))

    for off in (2, 1, 3):
        to = mod(x + off, X)
        xo[to] = combine(to).astype(BF16)
        x_sum(to).start()
    val = combine(x)
    for off in (1, 3, 2):
        frm = mod(x + off, X)
        x_summed(frm).wait_recv()
        val = val + xi[frm].astype(F32)

    first = h == 0
    zs[...] = jnp.where(first, val[:, quarter:], val[:, :quarter]).astype(BF16)
    last = remote(zs, zr, zss, zrs, other_z)
    last.start()
    keep = jnp.where(first, val[:, :quarter], val[:, quarter:])
    outs.append(weight_grad(gu, 2, gwu_h))
    last.wait_recv()
    gi[...] = (keep + zr[...].astype(F32)).astype(BF16)

    for off in (1, 2, 3):
        x_meta(off, x).wait_send()
        x_rows(off, x).wait_send()
        x_sum(mod(x + off, X)).wait_send()
    for off in range(1, Y):
        to = mod(y + off, Y)
        y_pass(to).wait_send()
        y_return(to).wait_send()
    for i in range(Y):
        core_pass(i).wait_send()
        core_sum(i).wait_send()

    def sent(ch, carry):
        add_in(ch).wait_send()

        @pl.when(pos > 0)
        def _():
            total_out(ch).wait_send()

        return carry

    lax.fori_loop(0, count, sent, 0)
    last.wait_send()
    for copy in outs:
        copy.wait()
    pltpu.make_async_copy(grad.at[0, pl.ds(0, width), :], gwd_h, out_sem.at[0]).wait()


def hand_over(a, b, c, d, ao, bo, co, do, av, bv, cv, dv, sem):
    for i, (src, via) in enumerate(((b, bv), (c, cv), (d, dv), (a, av))):
        pltpu.make_async_copy(src, via, sem.at[0, i]).start()
    for i, (src, via, dst) in enumerate(((b, bv, bo), (c, cv, co), (d, dv, do), (a, av, ao))):
        pltpu.make_async_copy(src, via, sem.at[0, i]).wait()
        pltpu.make_async_copy(via, dst, sem.at[1, i]).start()
    for i, (via, dst) in enumerate(((bv, bo), (cv, co), (dv, do), (av, ao))):
        pltpu.make_async_copy(via, dst, sem.at[1, i]).wait()


def per_device(
    grad_output, gate_probs, routes, saved_input, saved_gate, saved_up, w_gate, w_up, w_down
):
    tokens, width = grad_output.shape
    hidden = saved_gate.shape[2]
    count = Y * PIECES
    half, quarter = width // 2, width // 4
    dma = lambda *n: pltpu.SemaphoreType.DMA(n)
    vmem = pl.BlockSpec(memory_space=pltpu.VMEM)
    hbm = pl.BlockSpec(memory_space=pl.ANY)
    piece = (count, PIECE, hidden)
    results = (
        jax.ShapeDtypeStruct((tokens, quarter), BF16),
        jax.ShapeDtypeStruct((width, hidden), BF16),
        jax.ShapeDtypeStruct((width, hidden), BF16),
        jax.ShapeDtypeStruct((hidden, width), BF16),
    )
    outs = pl.pallas_call(
        kernel,
        out_shape=results,
        in_specs=[vmem] * 2 + [hbm] * 7,
        out_specs=(vmem, hbm, hbm, hbm),
        scratch_shapes=[
            pltpu.VMEM((X, ROWS, width), BF16),
            pltpu.VMEM((X, ROWS, hidden), BF16),
            pltpu.VMEM((X, ROWS, hidden), BF16),
            pltpu.VMEM((width, hidden), BF16),
            pltpu.VMEM((width, hidden), BF16),
            pltpu.VMEM((hidden, width), BF16),
            pltpu.VMEM((X, 16, tokens), F32),
            pltpu.VMEM((X, tokens, half), BF16),
            pltpu.VMEM((X, ROWS, tokens), F32),
            pltpu.VMEM((X, tokens, ROWS), F32),
            pltpu.VMEM((Y, BLOCK, half), F32),
            pltpu.VMEM((Y, BLOCK, half), BF16),
            pltpu.VMEM((2, Y, BLOCK, half), BF16),
            pltpu.VMEM(piece, BF16),
            pltpu.VMEM(piece, BF16),
            pltpu.VMEM(piece, BF16),
            pltpu.VMEM((Y, BLOCK, hidden), F32),
            pltpu.VMEM((Y, BLOCK, hidden), F32),
            pltpu.VMEM((Y, BLOCK, hidden), F32),
            pltpu.VMEM((Y, BLOCK, hidden), F32),
            pltpu.VMEM((Y, BLOCK, hidden), F32),
            pltpu.VMEM((Y, 2, 2, BLOCK, quarter), BF16),
            pltpu.VMEM((Y, 2, BLOCK, quarter), BF16),
            pltpu.VMEM((Y, 2, BLOCK, quarter), BF16),
            pltpu.VMEM((Y, 2, BLOCK, quarter), BF16),
            pltpu.VMEM((X, tokens, half), BF16),
            pltpu.VMEM((X, tokens, half), BF16),
            pltpu.VMEM((tokens, quarter), BF16),
            pltpu.VMEM((tokens, quarter), BF16),
            pltpu.VMEM((width, width), F32),
            pltpu.VMEM((3, width, width), BF16),
            dma(7), dma(3),
            dma(X), dma(X), dma(X), dma(X),
            dma(Y), dma(Y), dma(Y), dma(Y),
            dma(count), dma(count), dma(count), dma(count),
            dma(Y), dma(Y), dma(Y), dma(Y),
            dma(X), dma(X), pltpu.SemaphoreType.DMA, pltpu.SemaphoreType.DMA,
        ],
        compiler_params=pltpu.CompilerParams(
            collective_id=0, has_side_effects=True, vmem_limit_bytes=56 * 1024 * 1024
        ),
        cost_estimate=pl.CostEstimate(
            flops=10 * X * ROWS * width * hidden, bytes_accessed=6_000_000, transcendentals=X * ROWS * hidden
        ),
    )(
        routes.T, gate_probs.T, grad_output,
        saved_input.reshape(X, ROWS, width),
        saved_gate.reshape(X, ROWS, hidden), saved_up.reshape(X, ROWS, hidden),
        w_gate[0], w_up[0], w_down[0],
    )
    outs = pl.pallas_call(
        hand_over,
        out_shape=results,
        in_specs=[hbm] * 4,
        out_specs=(hbm,) * 4,
        scratch_shapes=[pltpu.VMEM(r.shape, BF16) for r in results] + [dma(2, 4)],
    )(*outs)
    return outs[0], outs[1][None], outs[2][None], outs[3][None]


def solution(mesh):
    placed = (
        P("expert", "dp"),
        P("expert", None),
        P("expert", None),
        P("expert", None, "dp"),
        P("expert", None, "tensor"),
        P("expert", None, "tensor"),
        P("expert", "dp", "tensor"),
        P("expert", "dp", "tensor"),
        P("expert", "tensor", "dp"),
    )
    return jax.shard_map(
        per_device,
        mesh=mesh,
        in_specs=placed,
        out_specs=(
            P("expert", ("dp", "tensor")),
            P("expert", "dp", "tensor"),
            P("expert", "dp", "tensor"),
            P("expert", "tensor", "dp"),
        ),
        check_vma=False,
    )
```

```python
import jax
import jax.numpy as jnp
from jax import lax
from jax.experimental import pallas as pl
from jax.experimental.pallas import tpu as pltpu
from jax.sharding import PartitionSpec as P

X = 4
Y = 8
CAP = 40
ROWS = Y * CAP
BLOCK = X * CAP
PIECES = 2
PIECE = BLOCK // PIECES
BF16 = jnp.bfloat16
F32 = jnp.float32
SLACK = 3


def mod(a, n):
    return lax.rem(a + 2 * n, n)


def turn(k):
    far = Y // 2 - k // 2
    return jnp.where(k == 0, 0, jnp.where((lax.rem(k, 2) == 1) & (k > 1), -far, far))


def dot(a, b, dims):
    return lax.dot_general(a, b, (dims, ((), ())), preferred_element_type=F32)


def kernel(
    routes, probs, go, sin_h, sg_h, su_h, wg_h, wu_h, wd_h,
    gi, gwg_h, gwu_h, gwd_h,
    sin, sg, su, wg, wu, wd,
    meta, gbuf, sel, selt, stage, ysend, arr, part, inb, tot, a1, a2, hid, gg, gu,
    pr, crecv, rsend, rret, xo, xi, zs, zr, acc, grad,
    load_sem, out_sem,
    ms, mr, gs, gr, ys_sem, yr_sem, cs, cr, ps, prs, ts, tr, ds, dr, qs, qr, xos, xis, zss, zrs,
):
    dp = lax.axis_index("dp")
    e = lax.axis_index("expert")
    t = lax.axis_index("tensor")
    x, y = e // Y, lax.rem(e, Y)
    h, c = t // 2, lax.rem(t, 2)
    n_dp = 8
    low = dp < n_dp // 2
    pos = jnp.where(low, dp, n_dp - 1 - dp)
    inward = jnp.where(low, dp + 1, dp - 1)
    outward = jnp.where(low, dp - 1, dp + 1)
    mid = n_dp // 2 - 1

    x_at = lambda xx: {"expert": xx * Y + y}
    y_at = lambda yy: {"expert": x * Y + yy}
    other_core = {"tensor": h * 2 + 1 - c}
    other_z = {"tensor": (1 - h) * 2 + c}
    at_in = {"dp": inward}
    at_out = {"dp": outward}

    barrier = pltpu.get_barrier_semaphore()

    def greet(where):
        pl.semaphore_signal(barrier, inc=1, device_id=where, device_id_type=pl.DeviceIdType.MESH)

    for off in (1, 2, 3):
        greet(x_at(mod(x + off, X)))
    for off in range(1, Y):
        greet(y_at(mod(y + off, Y)))
    for where in (other_core, other_z, at_in):
        greet(where)

    @pl.when(pos > 0)
    def _():
        greet(at_out)

    def remote(src, dst, ssem, rsem, where):
        return pltpu.make_async_remote_copy(
            src_ref=src, dst_ref=dst, send_sem=ssem, recv_sem=rsem,
            device_id=where, device_id_type=pl.DeviceIdType.MESH,
        )

    half = gbuf.shape[2]
    loads = [
        pltpu.make_async_copy(go.at[:, pl.ds(pl.multiple_of(c * half, half), half)], gbuf.at[x], load_sem.at[0])
    ]
    for i, (src, dst) in enumerate(((sg_h, sg), (su_h, su), (wd_h, wd), (wg_h, wg), (wu_h, wu), (sin_h, sin))):
        loads.append(pltpu.make_async_copy(src, dst, load_sem.at[i + 1]))
    for copy in loads:
        copy.start()

    meta[x, 0:8, :] = routes[...].astype(F32)
    meta[x, 8:16, :] = probs[...]
    tokens = routes.shape[1]
    loads[0].wait()
    pl.semaphore_wait(barrier, jnp.where(pos > 0, Y - 1 + 7, Y - 1 + 6))

    def x_meta(off, at):
        return remote(meta.at[at], meta.at[at], ms.at[off], mr.at[at], x_at(mod(x + off, X)))

    def x_rows(off, at):
        return remote(gbuf.at[at], gbuf.at[at], gs.at[off], gr.at[at], x_at(mod(x + off, X)))

    for off in (1, 3, 2):
        x_meta(off, x).start()
        x_rows(off, x).start()

    upper = (
        lax.broadcasted_iota(jnp.int32, (tokens, tokens), 0)
        < lax.broadcasted_iota(jnp.int32, (tokens, tokens), 1)
    ).astype(F32)
    names = (lax.broadcasted_iota(jnp.int32, (Y, tokens), 0) + x * Y).astype(F32)
    ranks_of = lax.broadcasted_iota(jnp.int32, (CAP, tokens), 0).astype(F32)

    def choose(block):
        named = meta[block, 0:8, :]
        weights = meta[block, 8:16, :]
        hits = jnp.zeros((Y, tokens), F32)
        weight = jnp.zeros((Y, tokens), F32)
        for k in range(8):
            same = named[k : k + 1, :] == names
            hits = hits + jnp.where(same, 1.0, 0.0)
            weight = weight + jnp.where(same, weights[k : k + 1, :], 0.0)
        rank = dot(hits, upper, ((1,), (0,)))
        rank = jnp.where(hits > 0.0, rank, -1.0)
        masks, scales = [], []
        for i in range(Y):
            mask = jnp.where(rank[i : i + 1, :] == ranks_of, 1.0, 0.0)
            masks.append(mask)
            scales.append(jnp.sum(mask * weight[i : i + 1, :], axis=1, keepdims=True))
        mask = jnp.concatenate(masks, axis=0)
        sel[block] = mask
        rows = dot(mask.astype(BF16), gbuf[block], ((1,), (0,))) * jnp.concatenate(scales, axis=0)
        at = pl.ds(pl.multiple_of(block * CAP, 8), CAP)
        for i in range(Y):
            stage[i, at, :] = rows[i * CAP : (i + 1) * CAP, :]

    choose(x)

    loads[1].wait()
    loads[2].wait()

    def activate(i, carry):
        gates = sg[i].astype(F32)
        ups = su[i].astype(F32)
        at = pl.ds(pl.multiple_of(i * CAP, 8), CAP)
        for yy in range(Y):
            gate = gates[yy * CAP : (yy + 1) * CAP, :]
            up = ups[yy * CAP : (yy + 1) * CAP, :]
            sig = jax.nn.sigmoid(gate)
            act = gate * sig
            a1[yy, at, :] = act
            a2[yy, at, :] = up * sig * (1.0 + gate * (1.0 - sig))
            hid[yy, at, :] = act * up
        return carry

    lax.fori_loop(0, X, activate, 0)

    for off in (1, 3, 2):
        xx = mod(x + off, X)
        x_meta(off, xx).wait_recv()
        x_rows(off, xx).wait_recv()
        choose(xx)

    def core_pass(yy):
        return remote(arr.at[c, yy], arr.at[c, yy], cs.at[yy], cr.at[yy], other_core)

    def core_arrival(yy):
        return remote(arr.at[1 - c, yy], arr.at[1 - c, yy], cs.at[yy], cr.at[yy], other_core)

    def y_pass(to):
        return remote(ysend.at[to], arr.at[c, y], ys_sem.at[to], yr_sem.at[y], y_at(to))

    def y_arrival(yy):
        return remote(ysend.at[yy], arr.at[c, yy], ys_sem.at[yy], yr_sem.at[yy], y_at(yy))

    arr[c, y] = stage[y].astype(BF16)
    core_pass(y).start()
    for off in (4, 3, -3, 2, -2, 1, -1):
        to = mod(y + off, Y)
        ysend[to] = stage[to].astype(BF16)
        y_pass(to).start()
    for copy in loads[3:]:
        copy.wait()

    def add_in(ch):
        return remote(part.at[ch], inb.at[ch], ps.at[ch], prs.at[ch], at_in)

    def add_mid(ch):
        return remote(part.at[ch], tot.at[ch], ps.at[ch], tr.at[ch], at_in)

    def total_out(ch):
        return remote(tot.at[ch], tot.at[ch], ts.at[ch], tr.at[ch], at_out)

    def core_sum(yy):
        return remote(pr.at[yy, 1 - c], crecv.at[yy], ds.at[yy], dr.at[yy], other_core)

    def y_return(yy):
        return remote(rsend.at[yy], rret.at[y], qs.at[yy], qr.at[y], y_at(yy))

    def y_returned(yy):
        return remote(rsend.at[yy], rret.at[yy], qs.at[yy], qr.at[yy], y_at(yy))

    count = Y * PIECES
    lag = SLACK * (2 * (mid - pos) + 1)
    width = wd.shape[0]

    def save(slot, value, result):
        rows, columns = value.shape
        where = grad.at[slot, pl.ds(0, rows), pl.ds(0, columns)]
        where[...] = value.astype(BF16)
        return pltpu.make_async_copy(where, result, out_sem.at[slot])

    def down_grad():
        part_acc = acc.at[pl.ds(0, width), :]

        def body(yy, carry):
            a = hid[yy].astype(BF16)
            for i in range(2):
                cut = slice(i * half, (i + 1) * half)
                term = dot(a, arr[i, yy], ((0,), (0,)))
                part_acc[:, cut] = jnp.where(yy == 0, term, part_acc[:, cut] + term)
            return carry

        lax.fori_loop(0, Y, body, 0)
        save(0, part_acc[...], gwd_h).start()

    def prepare():
        for i in range(X):
            selt[i] = sel[i].T.astype(BF16)
        down_grad()

    def step(s, carry):
        @pl.when(s < count)
        def _():
            k, q = s // PIECES, lax.rem(s, PIECES)
            yy = mod(y + turn(k), Y)
            ch = yy * PIECES + q

            @pl.when(q == 0)
            def _():
                core_arrival(yy).wait_recv()
                partial = dot(arr[0, yy], wd[:, :half], ((1,), (1,)))
                partial = partial + dot(arr[1, yy], wd[:, half:], ((1,), (1,)))
                for i in range(PIECES):
                    part[yy * PIECES + i] = partial[i * PIECE : (i + 1) * PIECE, :].astype(BF16)

            @pl.when(pos > 0)
            def _():
                add_in(ch).wait_recv()
                part[ch] = (part[ch].astype(F32) + inb[ch].astype(F32)).astype(BF16)

            @pl.when(pos < mid)
            def _():
                add_in(ch).start()

            @pl.when(pos == mid)
            def _():
                add_mid(ch).start()

            @pl.when((s >= 1) & (s < Y))
            def _():
                yn = mod(y + turn(s), Y)
                y_arrival(yn).wait_recv()
                core_pass(yn).start()

        @pl.when((s == count) & (pos == 0))
        def _():
            prepare()

        u = s - lag

        @pl.when((u >= 0) & (u < count))
        def _():
            k, q = u // PIECES, lax.rem(u + PIECES, PIECES)
            yy = mod(y + turn(k), Y)
            ch = yy * PIECES + q
            total_out(ch).wait_recv()

            @pl.when(pos == mid)
            def _():
                tot[ch] = (part[ch].astype(F32) + tot[ch].astype(F32)).astype(BF16)

            @pl.when(pos > 0)
            def _():
                total_out(ch).start()

            at = pl.ds(pl.multiple_of(q * PIECE, 8), PIECE)
            grad_hidden = tot[ch].astype(F32)
            gu[yy, at, :] = (grad_hidden * a1[yy, at, :]).astype(BF16).astype(F32)
            gg[yy, at, :] = (grad_hidden * a2[yy, at, :]).astype(BF16).astype(F32)

            @pl.when(q == PIECES - 1)
            def _():
                rows = dot(gg[yy].astype(BF16), wg[...], ((1,), (1,)))
                rows = rows + dot(gu[yy].astype(BF16), wu[...], ((1,), (1,)))
                quarter = rows.shape[1] // 4
                for i in range(4):
                    pr[yy, i % 2, i // 2] = rows[:, i * quarter : (i + 1) * quarter].astype(BF16)
                core_sum(yy).start()

        v = u - PIECES - 1

        @pl.when((v >= 0) & (lax.rem(v + PIECES * 64, PIECES) == 0))
        def _():
            yy = mod(y + turn(v // PIECES), Y)
            core_sum(yy).wait_recv()
            both = (pr[yy, c].astype(F32) + crecv[yy].astype(F32)).astype(BF16)

            @pl.when(yy == y)
            def _():
                rret[y] = both

            @pl.when(yy != y)
            def _():
                rsend[yy] = both
                y_return(yy).start()

        return carry

    lax.fori_loop(0, count + 2 + lag, step, 0)

    @pl.when(pos > 0)
    def _():
        prepare()

    def weight_grad(rows, slot, result):
        whole = acc.at[:, pl.ds(0, width)]

        def body(i, carry):
            at = pl.ds(pl.multiple_of(i * CAP, 8), CAP)
            b = jnp.concatenate([rows[yy, at, :] for yy in range(Y)], axis=0).astype(BF16)
            term = dot(sin[i], b, ((0,), (0,)))
            whole[...] = jnp.where(i == 0, term, whole[...] + term)
            return carry

        lax.fori_loop(0, X, body, 0)
        copy = save(slot, whole[...], result)
        copy.start()
        return copy


    quarter = rret.shape[3]
    for i in range(Y):
        yy = mod(y + turn(i), Y)

        @pl.when(yy != y)
        def _():
            y_returned(yy).wait_recv()

        for j in range(2):
            stage[yy, :, j * quarter : (j + 1) * quarter] = rret[yy, j].astype(F32)

    def combine(block):
        at = pl.ds(pl.multiple_of(block * CAP, 8), CAP)
        rows = jnp.concatenate([stage[i, at, :] for i in range(Y)], axis=0)
        return dot(selt[block], rows.astype(BF16), ((1,), (0,)))

    def x_sum(to):
        return remote(xo.at[to], xi.at[x], xos.at[to], xis.at[x], x_at(to))

    def x_summed(frm):
        return remote(xo.at[frm], xi.at[frm], xos.at[frm], xis.at[frm], x_at(frm))

    for off in (2, 1, 3):
        to = mod(x + off, X)
        xo[to] = combine(to).astype(BF16)
        x_sum(to).start()
    val = combine(x)
    outs = [weight_grad(gg, 1, gwg_h)]
    for off in (1, 3, 2):
        frm = mod(x + off, X)
        x_summed(frm).wait_recv()
        val = val + xi[frm].astype(F32)

    first = h == 0
    zs[...] = jnp.where(first, val[:, quarter:], val[:, :quarter]).astype(BF16)
    last = remote(zs, zr, zss, zrs, other_z)
    last.start()
    keep = jnp.where(first, val[:, :quarter], val[:, quarter:])
    outs.append(weight_grad(gu, 2, gwu_h))
    last.wait_recv()
    gi[...] = (keep + zr[...].astype(F32)).astype(BF16)

    for off in (1, 2, 3):
        x_meta(off, x).wait_send()
        x_rows(off, x).wait_send()
        x_sum(mod(x + off, X)).wait_send()
    for off in range(1, Y):
        to = mod(y + off, Y)
        y_pass(to).wait_send()
        y_return(to).wait_send()
    for i in range(Y):
        core_pass(i).wait_send()
        core_sum(i).wait_send()

    def sent(ch, carry):
        add_in(ch).wait_send()

        @pl.when(pos > 0)
        def _():
            total_out(ch).wait_send()

        return carry

    lax.fori_loop(0, count, sent, 0)
    last.wait_send()
    for copy in outs:
        copy.wait()
    pltpu.make_async_copy(grad.at[0, pl.ds(0, width), :], gwd_h, out_sem.at[0]).wait()


def hand_over(a, b, c, d, ao, bo, co, do, av, bv, cv, dv, sem):
    for i, (src, via) in enumerate(((b, bv), (c, cv), (d, dv), (a, av))):
        pltpu.make_async_copy(src, via, sem.at[0, i]).start()
    for i, (src, via, dst) in enumerate(((b, bv, bo), (c, cv, co), (d, dv, do), (a, av, ao))):
        pltpu.make_async_copy(src, via, sem.at[0, i]).wait()
        pltpu.make_async_copy(via, dst, sem.at[1, i]).start()
    for i, (via, dst) in enumerate(((bv, bo), (cv, co), (dv, do), (av, ao))):
        pltpu.make_async_copy(via, dst, sem.at[1, i]).wait()


def per_device(
    grad_output, gate_probs, routes, saved_input, saved_gate, saved_up, w_gate, w_up, w_down
):
    tokens, width = grad_output.shape
    hidden = saved_gate.shape[2]
    count = Y * PIECES
    half, quarter = width // 2, width // 4
    dma = lambda *n: pltpu.SemaphoreType.DMA(n)
    vmem = pl.BlockSpec(memory_space=pltpu.VMEM)
    hbm = pl.BlockSpec(memory_space=pl.ANY)
    piece = (count, PIECE, hidden)
    results = (
        jax.ShapeDtypeStruct((tokens, quarter), BF16),
        jax.ShapeDtypeStruct((width, hidden), BF16),
        jax.ShapeDtypeStruct((width, hidden), BF16),
        jax.ShapeDtypeStruct((hidden, width), BF16),
    )
    outs = pl.pallas_call(
        kernel,
        out_shape=results,
        in_specs=[vmem] * 2 + [hbm] * 7,
        out_specs=(vmem, hbm, hbm, hbm),
        scratch_shapes=[
            pltpu.VMEM((X, ROWS, width), BF16),
            pltpu.VMEM((X, ROWS, hidden), BF16),
            pltpu.VMEM((X, ROWS, hidden), BF16),
            pltpu.VMEM((width, hidden), BF16),
            pltpu.VMEM((width, hidden), BF16),
            pltpu.VMEM((hidden, width), BF16),
            pltpu.VMEM((X, 16, tokens), F32),
            pltpu.VMEM((X, tokens, half), BF16),
            pltpu.VMEM((X, ROWS, tokens), F32),
            pltpu.VMEM((X, tokens, ROWS), BF16),
            pltpu.VMEM((Y, BLOCK, half), F32),
            pltpu.VMEM((Y, BLOCK, half), BF16),
            pltpu.VMEM((2, Y, BLOCK, half), BF16),
            pltpu.VMEM(piece, BF16),
            pltpu.VMEM(piece, BF16),
            pltpu.VMEM(piece, BF16),
            pltpu.VMEM((Y, BLOCK, hidden), F32),
            pltpu.VMEM((Y, BLOCK, hidden), F32),
            pltpu.VMEM((Y, BLOCK, hidden), F32),
            pltpu.VMEM((Y, BLOCK, hidden), F32),
            pltpu.VMEM((Y, BLOCK, hidden), F32),
            pltpu.VMEM((Y, 2, 2, BLOCK, quarter), BF16),
            pltpu.VMEM((Y, 2, BLOCK, quarter), BF16),
            pltpu.VMEM((Y, 2, BLOCK, quarter), BF16),
            pltpu.VMEM((Y, 2, BLOCK, quarter), BF16),
            pltpu.VMEM((X, tokens, half), BF16),
            pltpu.VMEM((X, tokens, half), BF16),
            pltpu.VMEM((tokens, quarter), BF16),
            pltpu.VMEM((tokens, quarter), BF16),
            pltpu.VMEM((width, width), F32),
            pltpu.VMEM((3, width, width), BF16),
            dma(7), dma(3),
            dma(X), dma(X), dma(X), dma(X),
            dma(Y), dma(Y), dma(Y), dma(Y),
            dma(count), dma(count), dma(count), dma(count),
            dma(Y), dma(Y), dma(Y), dma(Y),
            dma(X), dma(X), pltpu.SemaphoreType.DMA, pltpu.SemaphoreType.DMA,
        ],
        compiler_params=pltpu.CompilerParams(
            collective_id=0, has_side_effects=True, vmem_limit_bytes=56 * 1024 * 1024
        ),
        cost_estimate=pl.CostEstimate(
            flops=10 * X * ROWS * width * hidden, bytes_accessed=6_000_000, transcendentals=X * ROWS * hidden
        ),
    )(
        routes.T, gate_probs.T, grad_output,
        saved_input.reshape(X, ROWS, width),
        saved_gate.reshape(X, ROWS, hidden), saved_up.reshape(X, ROWS, hidden),
        w_gate[0], w_up[0], w_down[0],
    )
    outs = pl.pallas_call(
        hand_over,
        out_shape=results,
        in_specs=[hbm] * 4,
        out_specs=(hbm,) * 4,
        scratch_shapes=[pltpu.VMEM(r.shape, BF16) for r in results] + [dma(2, 4)],
    )(*outs)
    return outs[0], outs[1][None], outs[2][None], outs[3][None]


def solution(mesh):
    placed = (
        P("expert", "dp"),
        P("expert", None),
        P("expert", None),
        P("expert", None, "dp"),
        P("expert", None, "tensor"),
        P("expert", None, "tensor"),
        P("expert", "dp", "tensor"),
        P("expert", "dp", "tensor"),
        P("expert", "tensor", "dp"),
    )
    return jax.shard_map(
        per_device,
        mesh=mesh,
        in_specs=placed,
        out_specs=(
            P("expert", ("dp", "tensor")),
            P("expert", "dp", "tensor"),
            P("expert", "dp", "tensor"),
            P("expert", "tensor", "dp"),
        ),
        check_vma=False,
    )
```
